128 devices in a mesh: days: 8 (over z, y_lo), space: 16 (over y_hi, x, core).
Axes of the slice: x: 4, y: 4 (y_hi: 2, y_lo: 2; y = y_hi * 2 + y_lo), z: 4, core: 2. Of those that a mesh axis runs over, the one named last changes fastest.
Arguments:
- targets: bfloat16 [1536, 4, 256, 128], P('days', None, 'space'), may hold values from -16 to 16, as said below
- archive: bfloat16 [384, 4, 256, 128], P('days', None, 'space'), may hold values from -6 to 6, as said below
- archive_fine: bfloat16 [384, 512, 256], P('days', 'space'), may hold values from -6 to 6
Outputs:
- downscaled: bfloat16 [1536, 512, 256], P('days', 'space')
The draws below stay inside these ranges and needn't reach their ends.
Inputs may be any that keep to these rules, and one draw needn't show every extreme that they name: `targets`: anomalies of the four fields. `archive`: anomalies of the four fields.
All inputs are finite; a program needn't handle non-finite values.
Results may differ from the reference program's by a relative error of at most 0.006.
Values may be sent and summed in bfloat16 or wider, within the bound.
A program may use at most 192 MiB of HBM per device.

```python
import jax
import jax.numpy as jnp
from jax import lax

CH = 4
BLOCK = 16
RIM = 8
COLS = 128
NROWS = 256
TARGETS = 1536
ARCHIVE = 384


def archive_field(key):
    base = jax.random.normal(jax.random.fold_in(key, 11), (ARCHIVE, CH, NROWS, COLS), jnp.float32)
    return jnp.clip(base, -6.0, 6.0)


def draw_archive(key, part):
    base = archive_field(key)
    return base.astype(jnp.bfloat16)


def draw_targets(key, part):
    own = jax.random.normal(jax.random.fold_in(key, 21), (TARGETS, CH, NROWS, COLS), jnp.float32)
    own = jnp.clip(own, -6.0, 6.0)
    return own.astype(jnp.bfloat16)


def block_levels(key, extent, shards, least, high):
    loudness, own = 1.0, jax.random.fold_in(key, 6)
    for dim, parts in shards:
        draws = jnp.exp(jax.random.uniform(jax.random.fold_in(own, dim), (parts,), jnp.float32, least / len(shards), high / len(shards)))
        loudness = loudness * jnp.repeat(draws, extent[dim] // parts).reshape([-1 if axis == dim else 1 for axis in range(len(extent))])
    return loudness


def bell_draw(stream_key, shape, spread, limit, shards=(), kind=jnp.bfloat16):
    array = spread * jax.random.normal(stream_key, shape, jnp.float32)
    if shards:
        array = array * block_levels(stream_key, shape, shards, -0.22, 0.18)
    return jnp.clip(array, -limit, limit).astype(kind)


def setup_inputs(seed: int = 0) -> dict:
    key_list = jax.random.split(jax.random.key(seed), 4)
    return {
        "targets": draw_targets(jax.random.fold_in(key_list[3], 71), 0),
        "archive": draw_archive(jax.random.fold_in(key_list[3], 71), 0),
        "archive_fine": bell_draw(key_list[2], (ARCHIVE, 2 * NROWS, 2 * COLS), 1.0, 6.0, ((0, 8), (1, 16))),
    }


def windows(cells):
    block_count = COLS // BLOCK
    day_count = cells.shape[0]
    padded = jnp.pad(cells, ((0, 0), (0, 0), (0, 0), (RIM, RIM)))
    split = padded.reshape(day_count, CH, 2 * BLOCK, block_count + 1, BLOCK)
    joined = jnp.concatenate([split[..., :block_count, :], split[..., 1:, :]], axis=-1)
    return jnp.transpose(joined, (0, 3, 1, 2, 4)).reshape(day_count, block_count, CH * 4 * BLOCK * BLOCK)


def reference(targets, archive, archive_fine):
    block_count = COLS // BLOCK
    target_padded = jnp.pad(targets, ((0, 0), (0, 0), (RIM, RIM), (0, 0)))
    archive_padded = jnp.pad(archive, ((0, 0), (0, 0), (RIM, RIM), (0, 0)))

    def one_row(row_block):
        first_row = (row_block * BLOCK).astype(jnp.int32)
        target_feat = windows(lax.dynamic_slice_in_dim(target_padded, first_row, 2 * BLOCK, 2)).astype(jnp.float32)
        archive_feat = windows(lax.dynamic_slice_in_dim(archive_padded, first_row, 2 * BLOCK, 2)).astype(jnp.float32)
        scores = jnp.einsum("tbf,abf->bta", target_feat, archive_feat) / 32.0
        peak_now = jnp.max(scores, axis=-1, keepdims=True)
        weights = jnp.exp(scores - peak_now)
        weight_sum = jnp.sum(weights, axis=-1)
        rounded = lax.optimization_barrier(weights.astype(jnp.bfloat16)).astype(jnp.float32)
        fine_rows = lax.dynamic_slice_in_dim(archive_fine, (row_block * 2 * BLOCK).astype(jnp.int32), 2 * BLOCK, 1)
        fine_blocks = fine_rows.reshape(ARCHIVE, 2 * BLOCK, block_count, 2 * BLOCK)
        fine_blocks = jnp.transpose(fine_blocks, (0, 2, 1, 3)).reshape(ARCHIVE, block_count, 4 * BLOCK * BLOCK).astype(jnp.float32)
        numerator = jnp.einsum("bta,abk->btk", rounded, fine_blocks)
        result = (numerator / weight_sum[..., None]).astype(jnp.bfloat16)
        result = result.reshape(block_count, TARGETS, 2 * BLOCK, 2 * BLOCK)
        return jnp.transpose(result, (1, 2, 0, 3)).reshape(TARGETS, 2 * BLOCK, 2 * COLS)

    stacked = lax.map(one_row, jnp.arange(NROWS // BLOCK, dtype=jnp.int32))
    return jnp.transpose(stacked, (1, 0, 2, 3)).reshape(TARGETS, 2 * NROWS, 2 * COLS)
```

```python
import functools

import jax
import jax.numpy as jnp
import ml_dtypes
import numpy as np
from jax import lax
from jax.experimental import pallas as pl
from jax.experimental.pallas import tpu as pltpu
from jax.sharding import PartitionSpec as P

MESH = pl.DeviceIdType.MESH
BF16, F32 = jnp.bfloat16, jnp.float32

NT, NA, NB = 192, 48, 8
ALL = 8 * NA
PIECE = 16

SENDS = {
    "y": [(0, 3, 0), (0, 3, 1), (0, 3, 2), (1, 4, 0), (2, 5, 0), (1, 4, 1), (2, 5, 1)],
    "z+": [(0, 2, 0), (0, 2, 1), (0, 2, 2), (2, 6, 0), (3, 5, 2), (2, 6, 1), (5, 7, 0)],
    "z-": [(0, 1, 0), (0, 1, 1), (0, 1, 2), (1, 6, 2), (3, 4, 2), (4, 7, 2), (4, 7, 1)],
}


def swap_matrix():
    m = np.zeros((16, 16, 16, 16), np.float32)
    for r in range(16):
        for t in range(16):
            m[r, t, t, r] = 1
    return m.reshape(256, 256).astype(ml_dtypes.bfloat16)


def cell_matrix():
    m = np.zeros((8, 128, 8, 8, 16), np.float32)
    for r in range(8):
        for j in range(8):
            for q in range(16):
                m[r, (16 * j - 8 + q) % 128, j, r, q] = 1
    return m.reshape(1024, 1024).astype(ml_dtypes.bfloat16)


def fine_matrix():
    m = np.zeros((4, 8, 32, 8, 4, 32), np.float32)
    for i in range(4):
        for b in range(8):
            for q in range(32):
                m[i, b, q, b, i, q] = 1
    return m.reshape(1024, 1024).astype(ml_dtypes.bfloat16)


def dot(a, b):
    return jnp.dot(a, b, preferred_element_type=F32)


def dot_t(a, b):
    return lax.dot_general(a, b, (((1,), (1,)), ((), ())), preferred_element_type=F32)


def gather_kernel(
    tgt_hbm, arc_hbm, fin_hbm, swap_ref, cellm_hbm, finem_hbm, out_hbm,
    t_raw, a_raw, f_raw, cellm, finem, ga, gf, tf, zbuf, own, xs, xr, relay, wts, inv, res,
    lsem, osem, gsend, grecv, xsend, xrecv, rsend, rrecv,
):
    d = lax.axis_index("days")
    s = lax.axis_index("space")
    z, y = d // 2, d % 2
    partner = 2 * z + 1 - y
    to = {"y": partner, "z+": 2 * lax.rem(z + 1, 4) + y, "z-": 2 * lax.rem(z + 3, 4) + y}

    up_direct = (s != 7) & (s != 15)
    down_direct = (s != 0) & (s != 8)
    is_edge = (s == 7) | (s == 8)
    low = s < 8
    is_relay = (low & (s % 2 == 1)) | (jnp.logical_not(low) & (s % 2 == 0))
    relay_to = jnp.where(low, 8, 7)
    relay_from = jnp.where(low, 7, 8)
    quarter = (s % 8) // 2
    first_relay = jnp.where(low, 1, 8)
    last_relay = jnp.where(low, 8, 1)

    barrier = pltpu.get_barrier_semaphore()

    def greet(day, space):
        pl.semaphore_signal(barrier, inc=1, device_id=(day, space), device_id_type=MESH)

    for link in to:
        greet(to[link], s)

    @pl.when(up_direct)
    def _():
        greet(d, s + 1)

    @pl.when(down_direct)
    def _():
        greet(d, s - 1)

    @pl.when(is_relay)
    def _():
        greet(partner, relay_from)

    @pl.when(is_edge)
    def _():
        for p in range(4):
            greet(partner, last_relay + 2 * p)

    loads = [
        pltpu.make_async_copy(src, dst, lsem.at[i])
        for i, (src, dst) in enumerate(
            [(arc_hbm, a_raw), (cellm_hbm, cellm), (finem_hbm, finem), (fin_hbm, f_raw), (tgt_hbm, t_raw)]
        )
    ]
    for load in loads:
        load.start()

    swap = swap_ref[...]
    lane = lax.broadcasted_iota(jnp.int32, (1, 128), 1) % 16
    right_half = jnp.where(lane >= 8, 1.0, 0.0).astype(BF16)
    left_half = jnp.where(lane < 8, 1.0, 0.0).astype(BF16)

    def cells(src, first, days, put):
        for tb in range(days // 16):
            for cp in range(2):
                x = jnp.concatenate(
                    [src[pl.ds(first + 16 * tb, 16), 2 * cp + c].reshape(256, 128) for c in range(2)], axis=1
                )
                w = dot(swap, x).astype(BF16)
                for c in range(2):
                    for r in range(16):
                        row = ((2 * cp + c) * 2 + r // 8) * days + 16 * tb
                        zbuf[pl.ds(row, 16), pl.ds((r % 8) * 128, 128)] = w[16 * r : 16 * r + 16, 128 * c : 128 * c + 128]
        for jp in range(4):
            o = dot(zbuf[pl.ds(0, 8 * days)], cellm[:, pl.ds(256 * jp, 256)]).astype(BF16)
            for c in range(4):
                for half in range(2):
                    row = (2 * c + half) * days
                    for jj in range(2):
                        put(half, 2 * jp + jj, c, o[row : row + days, 128 * jj : 128 * jj + 128])

    bufs = (ga, gf)

    def piece(arr, slot, p):
        return bufs[arr].at[:, pl.ds(slot * NA + p * PIECE, PIECE)]

    def remote(arr, link, there, src, dst, p):
        return pltpu.make_async_remote_copy(
            src_ref=piece(arr, src, p), dst_ref=piece(arr, dst, p),
            send_sem=gsend.at[arr, dst, p], recv_sem=grecv.at[arr, dst, p],
            device_id=(there, s), device_id_type=MESH,
        )

    arrived = {(arr, 0, p) for arr in range(2) for p in range(3)}
    sent = []

    def need(arr, slot, p):
        if (arr, slot, p) not in arrived:
            arrived.add((arr, slot, p))
            remote(arr, "y", partner, slot, slot, p).wait_recv()

    def send(arr, step):
        for link in to:
            src, dst, p = SENDS[link][step]
            need(arr, src, p)
            copy = remote(arr, link, to[link], src, dst, p)
            copy.start()
            sent.append(copy)

    def halo(row, k):
        there = s + 1 if row == 0 else s - 1
        return pltpu.make_async_remote_copy(
            src_ref=xs.at[row, k], dst_ref=xr.at[row, k],
            send_sem=xsend.at[row, k, 0], recv_sem=xrecv.at[row, k, 0],
            device_id=(d, there), device_id_type=MESH,
        )

    def halo_quarter(row, k, p):
        return pltpu.make_async_remote_copy(
            src_ref=xs.at[row, k, pl.ds(2 * p, 2)], dst_ref=relay.at[k],
            send_sem=xsend.at[row, k, p], recv_sem=rrecv.at[k],
            device_id=(partner, first_relay + 2 * p), device_id_type=MESH,
        )

    def pass_on(row, k, p):
        return pltpu.make_async_remote_copy(
            src_ref=relay.at[k], dst_ref=xr.at[row, k, pl.ds(2 * p, 2)],
            send_sem=rsend.at[k], recv_sem=xrecv.at[row, k, p],
            device_id=(partner, relay_to), device_id_type=MESH,
        )

    def halo_start(k):
        for row, direct, edge in ((0, up_direct, 7), (1, down_direct, 8)):
            @pl.when(direct)
            def _():
                halo(row, k).start()

            @pl.when(s == edge)
            def _():
                for p in range(4):
                    halo_quarter(row, k, p).start()

    def halo_pass(k):
        for row in range(2):
            @pl.when(is_relay & (low if row == 0 else jnp.logical_not(low)))
            def _():
                halo_quarter(row, k, 0).wait_recv()
                pass_on(row, k, quarter).start()

    def halo_wait(k):
        for row, direct, edge in ((0, down_direct, 8), (1, up_direct, 7)):
            @pl.when(direct)
            def _():
                halo(row, k).wait_recv()

            @pl.when(s == edge)
            def _():
                for p in range(4):
                    pass_on(row, k, p).wait_recv()

    def halo_drain(k):
        for row, direct, edge in ((0, up_direct, 7), (1, down_direct, 8)):
            @pl.when(direct)
            def _():
                halo(row, k).wait_send()

            @pl.when(s == edge)
            def _():
                for p in range(4):
                    halo_quarter(row, k, p).wait_send()

        @pl.when(is_relay)
        def _():
            pass_on(0, k, quarter).wait_send()

    def scores(k):
        days = pl.ds(128 * k, 128)

        @pl.loop(0, NB)
        def _(b):
            after = lax.rem(b + 1, NB)
            upper = dot_t(tf[b], ga[b, days]) + dot_t(tf[b + 1], ga[after, days])
            lower = dot_t(tf[9 + b], ga[8 + b, days]) + dot_t(tf[10 + b], ga[8 + after, days])
            own[k, b] = upper + lower
            xs[0, k, b] = lower
            xs[1, k, b] = upper

        halo_start(k)

    loads[0].wait()
    loads[1].wait()
    for p in range(3):
        def put(half, j, c, v):
            ga[8 * half + j, pl.ds(PIECE * p, PIECE), pl.ds(128 * c, 128)] = v

        cells(a_raw, PIECE * p, PIECE, put)
        if p == 0:
            pl.semaphore_wait(
                barrier,
                3 + up_direct.astype(jnp.int32) + down_direct.astype(jnp.int32)
                + is_relay.astype(jnp.int32) + 4 * is_edge.astype(jnp.int32),
            )
        send(0, p)

    loads[2].wait()
    loads[3].wait()
    for tb in range(3):
        for half in range(2):
            x = f_raw[pl.ds(16 * tb, 16), pl.ds(16 * half, 16)].reshape(256, 256)
            w = dot(swap, x).astype(BF16)
            for r in range(16):
                g, i = (16 * half + r) // 4, r % 4
                zbuf[pl.ds(NA * g + 16 * tb, 16), pl.ds(256 * i, 256)] = w[16 * r : 16 * r + 16]
    for bp in range(4):
        o = dot(zbuf[...], finem[:, pl.ds(256 * bp, 256)]).astype(BF16)
        for bb in range(2):
            for g in range(8):
                gf[2 * bp + bb, pl.ds(0, NA), pl.ds(128 * g, 128)] = o[NA * g : NA * g + NA, 128 * bb : 128 * bb + 128]

    loads[4].wait()

    @pl.loop(0, NT // NA)
    def _(n):
        first = pl.multiple_of(n * NA, NA)
        days = pl.ds(first, NA)

        def put(half, j, c, v):
            cols = pl.ds(128 * c, 128)
            if j:
                tf[9 * half + j, days, cols] = v
            else:
                tf[9 * half, days, cols] = v * right_half
                tf[9 * half + 8, days, cols] = v * left_half

        cells(t_raw, first, NA, put)

    for row, edge in ((0, 0), (1, 15)):
        @pl.when(s == edge)
        def _():
            xr[row] = jnp.zeros(xr.shape[1:], F32)

    def need_days(arr, lo, hi):
        for slot in range(8):
            for p in range(3):
                if lo <= slot * NA + p * PIECE < hi:
                    need(arr, slot, p)

    send(0, 3)
    need_days(0, 0, 128)
    scores(0)
    send(0, 4)
    send(0, 5)
    send(0, 6)
    send(1, 0)
    halo_pass(0)
    need_days(0, 128, 256)
    scores(1)
    send(1, 1)
    send(1, 2)
    need_days(0, 256, 384)
    scores(2)
    halo_pass(1)
    send(1, 3)
    send(1, 4)
    halo_pass(2)
    send(1, 5)
    for k in range(3):
        halo_wait(k)

    @pl.loop(0, NB)
    def _(b):
        x = [(own[k, b] + xr[0, k, b] + xr[1, k, b]) * (1.0 / 32.0) for k in range(3)]
        peak = jnp.max(jnp.maximum(jnp.maximum(x[0], x[1]), x[2]), axis=1, keepdims=True)
        e = [jnp.exp(v - peak) for v in x]
        total = jnp.sum(e[0] + e[1] + e[2], axis=1, keepdims=True)
        for k in range(3):
            wts[b, :, pl.ds(128 * k, 128)] = e[k].astype(BF16)
        inv[b] = jnp.broadcast_to(1.0 / total, (NT, 128))

    send(1, 6)
    need_days(1, 0, 384)

    def store(b):
        return pltpu.make_async_copy(res.at[b], out_hbm.at[b], osem.at[b])

    @pl.loop(0, NB)
    def _(b):
        scale = jnp.concatenate([inv[b], inv[b]], axis=1)
        for n in range(4):
            cols = pl.ds(256 * n, 256)
            res[b, :, cols] = (dot(wts[b], gf[b, :, cols]) * scale).astype(BF16)
        store(b).start()

    for k in range(3):
        halo_drain(k)
    for copy in sent:
        copy.wait_send()
    for b in range(NB):
        store(b).wait()


def lay_out_kernel(res_ref, finem_ref, swap_ref, out_ref, zbuf, rows):
    for g in range(8):
        for b in range(NB):
            zbuf[pl.ds(NA * g, NA), pl.ds(128 * b, 128)] = res_ref[b, :, pl.ds(128 * g, 128)]
    for i in range(4):
        o = dot_t(zbuf[...], finem_ref[pl.ds(256 * i, 256)]).astype(BF16)
        for g in range(8):
            rows[4 * g + i] = o[NA * g : NA * g + NA]
    for tb in range(3):
        for half in range(2):
            x = rows[pl.ds(16 * half, 16), pl.ds(16 * tb, 16)].reshape(256, 256)
            o = dot(swap_ref[...], x).astype(BF16)
            out_ref[pl.ds(16 * tb, 16), pl.ds(16 * half, 16)] = o.reshape(16, 16, 256)


def on_device(targets, archive, archive_fine):
    swap = jnp.asarray(swap_matrix())
    cellm = jnp.asarray(cell_matrix())
    finem = jnp.asarray(fine_matrix())
    hbm = pl.BlockSpec(memory_space=pl.ANY)
    vmem = pl.BlockSpec(memory_space=pltpu.VMEM)
    dma = pltpu.SemaphoreType.DMA
    res = pl.pallas_call(
        gather_kernel,
        out_shape=jax.ShapeDtypeStruct((NB, NT, 1024), BF16),
        in_specs=[hbm, hbm, hbm, vmem, hbm, hbm],
        out_specs=hbm,
        scratch_shapes=[
            pltpu.VMEM((NT, 4, 16, 128), BF16),
            pltpu.VMEM((NA, 4, 16, 128), BF16),
            pltpu.VMEM((NA, 32, 256), BF16),
            pltpu.VMEM((1024, 1024), BF16),
            pltpu.VMEM((1024, 1024), BF16),
            pltpu.VMEM((16, ALL, 512), BF16),
            pltpu.VMEM((NB, ALL, 1024), BF16),
            pltpu.VMEM((18, NT, 512), BF16),
            pltpu.VMEM((8 * NA, 1024), BF16),
            pltpu.VMEM((3, NB, NT, 128), F32),
            pltpu.VMEM((2, 3, NB, NT, 128), F32),
            pltpu.VMEM((2, 3, NB, NT, 128), F32),
            pltpu.VMEM((3, 2, NT, 128), F32),
            pltpu.VMEM((NB, NT, ALL), BF16),
            pltpu.VMEM((NB, NT, 128), F32),
            pltpu.VMEM((NB, NT, 1024), BF16),
            dma((5,)), dma((NB,)), dma((2, 8, 3)), dma((2, 8, 3)),
            dma((2, 3, 4)), dma((2, 3, 4)), dma((3,)), dma((3,)),
        ],
        compiler_params=pltpu.CompilerParams(
            collective_id=0, has_side_effects=True, vmem_limit_bytes=60 << 20
        ),
        cost_estimate=pl.CostEstimate(flops=6_000_000_000, bytes_accessed=16_000_000, transcendentals=600_000),
    )(targets, archive, archive_fine, swap, cellm, finem)
    return pl.pallas_call(
        lay_out_kernel,
        grid=(NT // NA,),
        out_shape=jax.ShapeDtypeStruct((NT, 32, 256), BF16),
        in_specs=[
            pl.BlockSpec((NB, NA, 1024), lambda n: (0, n, 0)),
            pl.BlockSpec((1024, 1024), lambda n: (0, 0)),
            pl.BlockSpec((256, 256), lambda n: (0, 0)),
        ],
        out_specs=pl.BlockSpec((NA, 32, 256), lambda n: (n, 0, 0)),
        scratch_shapes=[pltpu.VMEM((8 * NA, 1024), BF16), pltpu.VMEM((32, NA, 256), BF16)],
        compiler_params=pltpu.CompilerParams(vmem_limit_bytes=40 << 20),
        cost_estimate=pl.CostEstimate(flops=4_000_000_000, bytes_accessed=8_000_000, transcendentals=0),
    )(res, finem, swap)


def solution(mesh):
    return jax.shard_map(
        on_device,
        mesh=mesh,
        in_specs=(
            P("days", None, "space", None),
            P("days", None, "space", None),
            P("days", "space", None),
        ),
        out_specs=P("days", "space", None),
        check_vma=False,
    )
```

```python
import functools

import jax
import jax.numpy as jnp
import ml_dtypes
import numpy as np
from jax import lax
from jax.experimental import pallas as pl
from jax.experimental.pallas import tpu as pltpu
from jax.sharding import PartitionSpec as P

MESH = pl.DeviceIdType.MESH
BF16, F32 = jnp.bfloat16, jnp.float32

NT, NA, NB = 192, 48, 8
ALL = 8 * NA

HEAD = [
    (0, "y", 0, 3, 0), (0, "z-", 0, 1, 0), (0, "z+", 0, 2, 3),
    (0, "z-", 0, 1, 3), (0, "z+", 0, 2, 0), (0, "y", 0, 3, 1),
    (0, "z+", 0, 2, 1), (0, "y", 0, 3, 2), (0, "z-", 0, 1, 2),
]
SENDS = [
    (0, "y", 1, 4, 0), (0, "z+", 3, 5, 0), (0, "z-", 1, 6, 0),
    (0, "z+", 0, 2, 2), (0, "y", 2, 5, 3), (0, "z-", 3, 4, 1),
    (1, "z-", 0, 1, 0), (0, "y", 2, 5, 1), (0, "z+", 2, 6, 1),
    (0, "y", 1, 4, 2), (0, "z+", 3, 5, 2), (0, "z-", 4, 7, 0),
    (0, "y", 0, 3, 3), (0, "z-", 0, 1, 1), (0, "z+", 5, 7, 3),
    (1, "y", 1, 4, 0), (0, "z+", 5, 7, 1), (0, "z-", 1, 6, 2),
    "scores 0",
    (0, "y", 1, 4, 3), (0, "z+", 2, 6, 3), (0, "z-", 4, 7, 2),
    (1, "y", 0, 3, 2), (1, "z+", 0, 2, 1), (1, "z-", 0, 1, 2),
    "scores 1",
    (1, "y", 0, 3, 0), (1, "z+", 0, 2, 3), (1, "z-", 4, 7, 0),
    "scores 2", "scores 3",
    (1, "y", 0, 3, 1), (1, "z+", 0, 2, 2), (1, "z-", 0, 1, 1),
    "pass 0",
    (1, "y", 2, 5, 1), (1, "z+", 0, 2, 0), (1, "z-", 1, 6, 2),
    "pass 1",
    (1, "y", 1, 4, 2), (1, "z+", 3, 5, 0), (1, "z-", 1, 6, 0),
    "pass 2",
    (1, "y", 2, 5, 3), (1, "z+", 2, 6, 1), (1, "z-", 0, 1, 3),
    "pass 3", "weights 0",
    (1, "y", 0, 3, 3), (1, "z+", 5, 7, 1), (1, "z-", 3, 4, 1),
    "weights 1",
    (1, "y", 1, 4, 3), (1, "z+", 3, 5, 2), (1, "z-", 4, 7, 2),
    "weights 2", "result 0",
    (1, "z+", 5, 7, 3), (1, "z-", 1, 6, 3),
    "weights 3", "result 1", "result 2", "result 3",
]
GROUPS = [(0, 1), (1, 3), (3, 5), (5, 8)]


def swap_matrix():
    m = np.zeros((16, 16, 16, 16), np.float32)
    for r in range(16):
        for t in range(16):
            m[r, t, t, r] = 1
    return m.reshape(256, 256).astype(ml_dtypes.bfloat16)


def cell_matrix():
    m = np.zeros((8, 128, 8, 8, 16), np.float32)
    for r in range(8):
        for j in range(8):
            for q in range(16):
                m[r, (16 * j - 8 + q) % 128, j, r, q] = 1
    return m.reshape(1024, 1024).astype(ml_dtypes.bfloat16)


def fine_matrix():
    m = np.zeros((4, 4, 32, 4, 4, 32), np.float32)
    for i in range(4):
        for b in range(4):
            for q in range(32):
                m[i, b, q, b, i, q] = 1
    return m.reshape(512, 512).astype(ml_dtypes.bfloat16)


def dot(a, b):
    return jnp.dot(a, b, preferred_element_type=F32)


def dot_t(a, b):
    return lax.dot_general(a, b, (((1,), (1,)), ((), ())), preferred_element_type=F32)


def gather_kernel(
    tgt_hbm, arc_hbm, fin_hbm, swap_hbm, cellm_hbm, finem_hbm, rows,
    t_raw, a_raw, f_raw, swap_ref, cellm, finem, ga, gf, tf, zbuf, own, xs, xr, relay, wts, inv, res,
    lsem, gsend, grecv, xsend, xrecv, rsend, rrecv,
):
    d = lax.axis_index("days")
    s = lax.axis_index("space")
    z, y = d // 2, d % 2
    partner = 2 * z + 1 - y
    to = {"y": partner, "z+": 2 * lax.rem(z + 1, 4) + y, "z-": 2 * lax.rem(z + 3, 4) + y}

    up_direct = (s != 7) & (s != 15)
    down_direct = (s != 0) & (s != 8)
    is_edge = (s == 7) | (s == 8)
    low = s < 8
    is_relay = (low & (s % 2 == 1)) | (jnp.logical_not(low) & (s % 2 == 0))
    relay_to = jnp.where(low, 8, 7)
    relay_from = jnp.where(low, 7, 8)
    quarter = (s % 8) // 2
    first_relay = jnp.where(low, 1, 8)
    last_relay = jnp.where(low, 8, 1)

    loads = [
        pltpu.make_async_copy(src, dst, lsem.at[i])
        for i, (src, dst) in enumerate(
            [
                (arc_hbm, a_raw), (swap_hbm, swap_ref), (cellm_hbm, cellm),
                (finem_hbm, finem), (fin_hbm, f_raw), (tgt_hbm, t_raw),
            ]
        )
    ]
    for load in loads:
        load.start()

    barrier = pltpu.get_barrier_semaphore()

    def greet(day, space):
        pl.semaphore_signal(barrier, inc=1, device_id=(day, space), device_id_type=MESH)

    for link in to:
        greet(to[link], s)

    @pl.when(up_direct)
    def _():
        greet(d, s + 1)

    @pl.when(down_direct)
    def _():
        greet(d, s - 1)

    @pl.when(is_relay)
    def _():
        greet(partner, relay_from)

    @pl.when(is_edge)
    def _():
        for p in range(4):
            greet(partner, last_relay + 2 * p)

    lane = lax.broadcasted_iota(jnp.int32, (1, 128), 1) % 16
    right_half = jnp.where(lane >= 8, 1.0, 0.0).astype(BF16)
    left_half = jnp.where(lane < 8, 1.0, 0.0).astype(BF16)

    def cell_rows(src, first):
        for tb in range(3):
            for cp in range(2):
                x = jnp.concatenate(
                    [src[pl.ds(first + 16 * tb, 16), 2 * cp + c].reshape(256, 128) for c in range(2)], axis=1
                )
                w = dot(swap_ref[...], x).astype(BF16)
                for c in range(2):
                    for r in range(16):
                        row = ((2 * cp + c) * 2 + r // 8) * NA + 16 * tb
                        zbuf[pl.ds(row, 16), pl.ds((r % 8) * 128, 128)] = w[16 * r : 16 * r + 16, 128 * c : 128 * c + 128]

    def supercells(jp, put):
        o = dot(zbuf[...], cellm[:, pl.ds(256 * jp, 256)]).astype(BF16)
        for c in range(4):
            for half in range(2):
                row = (2 * c + half) * NA
                for jj in range(2):
                    put(half, 2 * jp + jj, c, o[row : row + NA, 128 * jj : 128 * jj + 128])

    bufs = (ga, gf)
    wide = (4, 2)

    def piece(arr, slot, p):
        return bufs[arr].at[pl.ds(wide[arr] * p, wide[arr]), pl.ds(slot * NA, NA)]

    def remote(arr, link, src, dst, p):
        return pltpu.make_async_remote_copy(
            src_ref=piece(arr, src, p), dst_ref=piece(arr, dst, p),
            send_sem=gsend.at[arr, dst, p], recv_sem=grecv.at[arr, dst, p],
            device_id=(to[link], s), device_id_type=MESH,
        )

    arrived = {(arr, 0, p) for arr in range(2) for p in range(4)}
    sent = []

    def need(arr, slot, p):
        if (arr, slot, p) not in arrived:
            arrived.add((arr, slot, p))
            remote(arr, "y", slot, slot, p).wait_recv()

    def send(arr, link, src, dst, p):
        need(arr, src, p)
        copy = remote(arr, link, src, dst, p)
        copy.start()
        sent.append(copy)

    def blocks_of(k):
        return pl.ds(GROUPS[k][0], GROUPS[k][1] - GROUPS[k][0])

    def halo(row, k):
        there = s + 1 if row == 0 else s - 1
        return pltpu.make_async_remote_copy(
            src_ref=xs.at[row, blocks_of(k)], dst_ref=xr.at[row, blocks_of(k)],
            send_sem=xsend.at[row, k, 0], recv_sem=xrecv.at[row, k, 0],
            device_id=(d, there), device_id_type=MESH,
        )

    def halo_quarter(row, k, p):
        return pltpu.make_async_remote_copy(
            src_ref=xs.at[row, blocks_of(k), pl.ds(NA * p, NA)], dst_ref=relay.at[blocks_of(k)],
            send_sem=xsend.at[row, k, p], recv_sem=rrecv.at[k],
            device_id=(partner, first_relay + 2 * p), device_id_type=MESH,
        )

    def pass_on(row, k, p):
        if not isinstance(p, int):
            first = pl.multiple_of(NA * p, NA)
        else:
            first = NA * p
        return pltpu.make_async_remote_copy(
            src_ref=relay.at[blocks_of(k)], dst_ref=xr.at[row, blocks_of(k), pl.ds(first, NA)],
            send_sem=rsend.at[k], recv_sem=xrecv.at[row, k, p],
            device_id=(partner, relay_to), device_id_type=MESH,
        )

    def halo_start(k):
        for row, direct, edge in ((0, up_direct, 7), (1, down_direct, 8)):
            @pl.when(direct)
            def _():
                halo(row, k).start()

            @pl.when(s == edge)
            def _():
                for p in range(4):
                    halo_quarter(row, k, p).start()

    def halo_pass(k):
        for row in range(2):
            @pl.when(is_relay & (low if row == 0 else jnp.logical_not(low)))
            def _():
                halo_quarter(row, k, 0).wait_recv()
                pass_on(row, k, quarter).start()

    def halo_wait(k):
        for row, direct, edge in ((0, down_direct, 8), (1, up_direct, 7)):
            @pl.when(direct)
            def _():
                halo(row, k).wait_recv()

            @pl.when(s == edge)
            def _():
                for p in range(4):
                    pass_on(row, k, p).wait_recv()

    def halo_drain(k):
        for row, direct, edge in ((0, up_direct, 7), (1, down_direct, 8)):
            @pl.when(direct)
            def _():
                halo(row, k).wait_send()

            @pl.when(s == edge)
            def _():
                for p in range(4):
                    halo_quarter(row, k, p).wait_send()

        @pl.when(is_relay)
        def _():
            pass_on(0, k, quarter).wait_send()

    def scores(k):
        for slot in range(8):
            need(0, slot, k)

        @pl.loop(*GROUPS[k])
        def _(b):
            after = lax.rem(b + 1, NB)
            upper = dot_t(tf[b], ga[2 * b]) + dot_t(tf[b + 1], ga[2 * after])
            lower = dot_t(tf[9 + b], ga[2 * b + 1]) + dot_t(tf[10 + b], ga[2 * after + 1])
            own[b] = upper + lower
            xs[0, b] = lower
            xs[1, b] = upper

        halo_start(k)

    def weights(k):
        halo_wait(k)

        @pl.loop(*GROUPS[k])
        def _(b):
            for n in range(2):
                days = pl.ds(96 * n, 96)
                x = (own[b, days] + xr[0, b, days] + xr[1, b, days]) * (1.0 / 32.0)
                e = jnp.exp(x - jnp.max(x, axis=1, keepdims=True))
                wts[b, days] = e.astype(BF16)
                inv[b, days] = jnp.broadcast_to(1.0 / jnp.sum(e, axis=1, keepdims=True), (96, 128))

    def result(p):
        for slot in range(8):
            need(1, slot, p)

        @pl.loop(2 * p, 2 * p + 2)
        def _(b):
            scale = jnp.concatenate([inv[b], inv[b]], axis=1)
            for n in range(4):
                cols = pl.ds(256 * n, 256)
                res[b, :, cols] = (dot(wts[b], gf[b, :, cols]) * scale).astype(BF16)

        if p % 2:
            side = p // 2
            for g in range(8):
                x = jnp.concatenate([res[4 * side + b, :, pl.ds(128 * g, 128)] for b in range(4)], axis=1)
                o = dot(x, finem[...]).astype(BF16)
                for i in range(4):
                    rows[4 * g + i, :, pl.ds(128 * side, 128)] = o[:, 128 * i : 128 * i + 128]

    def put_archive(half, j, c, v):
        ga[2 * j + half, pl.ds(0, NA), pl.ds(128 * c, 128)] = v

    loads[0].wait()
    loads[1].wait()
    cell_rows(a_raw, 0)
    loads[2].wait()
    supercells(0, put_archive)
    pl.semaphore_wait(
        barrier,
        3 + up_direct.astype(jnp.int32) + down_direct.astype(jnp.int32)
        + is_relay.astype(jnp.int32) + 4 * is_edge.astype(jnp.int32),
    )
    laid = {0}
    for item in HEAD:
        if item[4] not in laid:
            laid.add(item[4])
            supercells(item[4], put_archive)
        send(*item)

    loads[3].wait()
    loads[4].wait()
    for tb in range(3):
        for half in range(2):
            x = f_raw[pl.ds(16 * tb, 16), pl.ds(16 * half, 16)].reshape(256, 256)
            w = dot(swap_ref[...], x).astype(BF16)
            for r in range(16):
                g, i = (16 * half + r) // 4, r % 4
                for side in range(2):
                    zbuf[pl.ds(NA * g + 16 * tb, 16), pl.ds(512 * side + 128 * i, 128)] = w[
                        16 * r : 16 * r + 16, 128 * side : 128 * side + 128
                    ]
    for side in range(2):
        o = dot(zbuf[:, pl.ds(512 * side, 512)], finem[...]).astype(BF16)
        for b in range(4):
            for g in range(8):
                gf[4 * side + b, pl.ds(0, NA), pl.ds(128 * g, 128)] = o[NA * g : NA * g + NA, 128 * b : 128 * b + 128]

    loads[5].wait()

    def targets(lo, hi):
        @pl.loop(lo, hi)
        def _(n):
            first = pl.multiple_of(n * NA, NA)
            days = pl.ds(first, NA)

            def put(half, j, c, v):
                cols = pl.ds(128 * c, 128)
                if j:
                    tf[9 * half + j, days, cols] = v
                else:
                    tf[9 * half, days, cols] = v * right_half
                    tf[9 * half + 8, days, cols] = v * left_half

            cell_rows(t_raw, first)
            for jp in range(4):
                supercells(jp, put)

    targets(0, 2)
    for item in SENDS[:6]:
        send(*item)
    targets(2, 4)

    for row, edge in ((0, 0), (1, 15)):
        @pl.when(s == edge)
        def _():
            xr[row] = jnp.zeros(xr.shape[1:], F32)

    todo = {"scores": scores, "pass": halo_pass, "weights": weights, "result": result}
    for item in SENDS[6:]:
        if isinstance(item, str):
            name, k = item.split()
            todo[name](int(k))
        else:
            send(*item)

    for k in range(4):
        halo_drain(k)
    for copy in sent:
        copy.wait_send()


def lay_out_kernel(rows_ref, swap_ref, out_ref):
    for tb in range(6):
        for half in range(2):
            x = rows_ref[pl.ds(16 * half, 16), pl.ds(16 * tb, 16)].reshape(256, 256)
            o = dot(swap_ref[...], x).astype(BF16)
            out_ref[pl.ds(16 * tb, 16), pl.ds(16 * half, 16)] = o.reshape(16, 16, 256)


def on_device(targets, archive, archive_fine):
    swap = jnp.asarray(swap_matrix())
    cellm = jnp.asarray(cell_matrix())
    finem = jnp.asarray(fine_matrix())
    hbm = pl.BlockSpec(memory_space=pl.ANY)
    vmem = pl.BlockSpec(memory_space=pltpu.VMEM)
    dma = pltpu.SemaphoreType.DMA
    rows = pl.pallas_call(
        gather_kernel,
        out_shape=pltpu.VMEM((32, NT, 256), BF16),
        in_specs=[hbm] * 6,
        out_specs=vmem,
        scratch_shapes=[
            pltpu.VMEM((NT, 4, 16, 128), BF16),
            pltpu.VMEM((NA, 4, 16, 128), BF16),
            pltpu.VMEM((NA, 32, 256), BF16),
            pltpu.VMEM((256, 256), BF16),
            pltpu.VMEM((1024, 1024), BF16),
            pltpu.VMEM((512, 512), BF16),
            pltpu.VMEM((16, ALL, 512), BF16),
            pltpu.VMEM((NB, ALL, 1024), BF16),
            pltpu.VMEM((18, NT, 512), BF16),
            pltpu.VMEM((8 * NA, 1024), BF16),
            pltpu.VMEM((NB, NT, ALL), F32),
            pltpu.VMEM((2, NB, NT, ALL), F32),
            pltpu.VMEM((2, NB, NT, ALL), F32),
            pltpu.VMEM((NB, NA, ALL), F32),
            pltpu.VMEM((NB, NT, ALL), BF16),
            pltpu.VMEM((NB, NT, 128), F32),
            pltpu.VMEM((NB, NT, 1024), BF16),
            dma((6,)), dma((2, 8, 4)), dma((2, 8, 4)),
            dma((2, 4, 4)), dma((2, 4, 4)), dma((4,)), dma((4,)),
        ],
        compiler_params=pltpu.CompilerParams(
            collective_id=0, has_side_effects=True, vmem_limit_bytes=56 << 20
        ),
        cost_estimate=pl.CostEstimate(flops=6_000_000_000, bytes_accessed=16_000_000, transcendentals=600_000),
    )(*[
        pltpu.with_memory_space_constraint(x, pltpu.HBM)
        for x in (targets, archive, archive_fine, swap, cellm, finem)
    ])
    return pl.pallas_call(
        lay_out_kernel,
        grid=(NT // 96,),
        out_shape=jax.ShapeDtypeStruct((NT, 32, 256), BF16),
        in_specs=[
            pl.BlockSpec((32, 96, 256), lambda n: (0, n, 0)),
            pl.BlockSpec((256, 256), lambda n: (0, 0)),
        ],
        out_specs=pl.BlockSpec((96, 32, 256), lambda n: (n, 0, 0)),
        compiler_params=pltpu.CompilerParams(vmem_limit_bytes=32 << 20),
        cost_estimate=pl.CostEstimate(flops=800_000_000, bytes_accessed=6_300_000, transcendentals=0),
    )(rows, swap)


def solution(mesh):
    return jax.shard_map(
        on_device,
        mesh=mesh,
        in_specs=(
            P("days", None, "space", None),
            P("days", None, "space", None),
            P("days", "space", None),
        ),
        out_specs=P("days", "space", None),
        check_vma=False,
    )
```

```python
import functools

import jax
import jax.numpy as jnp
import ml_dtypes
import numpy as np
from jax import lax
from jax.experimental import pallas as pl
from jax.experimental.pallas import tpu as pltpu
from jax.sharding import PartitionSpec as P

MESH = pl.DeviceIdType.MESH
BF16, F32 = jnp.bfloat16, jnp.float32

NT, NA, NB = 192, 48, 8
ALL = 8 * NA

HEAD = [
    (0, "y", 0, 3, 0), (0, "z+", 0, 2, 1), (0, "z-", 0, 1, 0), (0, "y", 0, 3, 1), (0, "z+", 0, 2, 0),
    (0, "z-", 0, 1, 2), (0, "y", 1, 4, 0), (0, "z+", 0, 2, 3), (0, "z-", 1, 6, 0),
]
SENDS = [
    (0, "y", 2, 5, 1), (0, "z+", 3, 5, 0), (0, "z-", 0, 1, 1), (0, "y", 0, 3, 2), (0, "z+", 2, 6, 1),
    (0, "z-", 4, 7, 0), (0, "y", 1, 4, 2), (0, "z+", 5, 7, 1), (1, "z-", 0, 1, 0), (0, "z-", 3, 4, 1),
    "scores 0", (1, "y", 0, 3, 0), (1, "z+", 0, 2, 1), (0, "y", 2, 5, 3), (0, "z-", 0, 1, 3),
    (0, "z+", 0, 2, 2), "scores 1", (0, "z-", 1, 6, 2), (1, "y", 1, 4, 0), (0, "z+", 3, 5, 2), "pass 0",
    (0, "z-", 4, 7, 2), (0, "y", 0, 3, 3), (0, "z+", 2, 6, 3), (1, "z-", 1, 6, 0), "pass 1", (0, "y", 1, 4, 3),
    (0, "z+", 5, 7, 3), "scores 2", (1, "z-", 4, 7, 0), (1, "y", 0, 3, 1), (1, "z+", 0, 2, 0),
    (1, "z+", 0, 2, 3), (1, "z-", 0, 1, 2), "weights 0", "scores 3", "lay 2", (1, "y", 2, 5, 1),
    (1, "z+", 3, 5, 0), (1, "z-", 0, 1, 1), "weights 1", "lay 3", "pass 2", (1, "z+", 2, 6, 1),
    (1, "z-", 3, 4, 1), (1, "y", 1, 4, 2), "lay 1", "lay 5", (1, "z+", 5, 7, 1), (1, "z-", 0, 1, 3), "pass 3",
    (1, "y", 0, 3, 2), "lay 4", "lay 6", (1, "z+", 0, 2, 2), (1, "z-", 1, 6, 2), (1, "y", 2, 5, 3), "lay 7",
    "result 0", "weights 2", "result 1", (1, "z-", 4, 7, 2), (1, "z+", 3, 5, 2), (1, "y", 0, 3, 3),
    (1, "z-", 1, 6, 3), (1, "z+", 5, 7, 3), (1, "y", 1, 4, 3), "weights 3", "result 2", "result 3",
]
GROUPS = [(0, 1), (1, 3), (3, 5), (5, 8)]


def swap_matrix():
    m = np.zeros((16, 16, 16, 16), np.float32)
    for r in range(16):
        for t in range(16):
            m[r, t, t, r] = 1
    return m.reshape(256, 256).astype(ml_dtypes.bfloat16)


def cell_matrix():
    m = np.zeros((8, 128, 8, 8, 16), np.float32)
    for r in range(8):
        for j in range(8):
            for q in range(16):
                m[r, (16 * j - 8 + q) % 128, j, r, q] = 1
    return m.reshape(1024, 1024).astype(ml_dtypes.bfloat16)


def fine_matrix():
    m = np.zeros((4, 4, 32, 4, 4, 32), np.float32)
    for i in range(4):
        for b in range(4):
            for q in range(32):
                m[i, b, q, b, i, q] = 1
    return m.reshape(512, 512).astype(ml_dtypes.bfloat16)


def dot(a, b):
    return jnp.dot(a, b, preferred_element_type=F32)


def dot_t(a, b):
    return lax.dot_general(a, b, (((1,), (1,)), ((), ())), preferred_element_type=F32)


def gather_kernel(
    tgt_hbm, arc_hbm, fin_hbm, swap_hbm, cellm_hbm, finem_hbm, rows,
    t_raw, a_raw, f_raw, f_left, swap_ref, cellm, finem, ga, gf, tf, zbuf, own, xs, xr, relay, wts, inv, res,
    lsem, gsend, grecv, xsend, xrecv, rsend, rrecv, esend, erecv,
):
    d = lax.axis_index("days")
    s = lax.axis_index("space")
    z, y = d // 2, d % 2
    partner = 2 * z + 1 - y
    to = {"y": partner, "z+": 2 * lax.rem(z + 1, 4) + y, "z-": 2 * lax.rem(z + 3, 4) + y}

    up_direct = (s != 7) & (s != 15)
    down_direct = (s != 0) & (s != 8)
    is_edge = (s == 7) | (s == 8)
    low = s < 8
    is_relay = (low & (s % 2 == 1)) | (jnp.logical_not(low) & (s % 2 == 0))
    relay_to = jnp.where(low, 8, 7)
    relay_from = jnp.where(low, 7, 8)
    quarter = (s % 8) // 2
    first_relay = jnp.where(low, 1, 8)
    last_relay = jnp.where(low, 8, 1)

    loads = [
        pltpu.make_async_copy(src, dst, lsem.at[i])
        for i, (src, dst) in enumerate(
            [
                (arc_hbm, a_raw), (swap_hbm, swap_ref), (cellm_hbm, cellm),
                (finem_hbm, finem),
                (fin_hbm.at[:, pl.ds(0, 16), pl.ds(0, 128)], f_left.at[0, 0]),
                (fin_hbm.at[:, pl.ds(16, 16), pl.ds(0, 128)], f_left.at[1, 0]),
                (fin_hbm.at[:, pl.ds(0, 16), pl.ds(128, 128)], f_raw.at[0]),
                (fin_hbm.at[:, pl.ds(16, 16), pl.ds(128, 128)], f_raw.at[1]),
                (tgt_hbm, t_raw),
            ]
        )
    ]
    for load in loads:
        load.start()

    barrier = pltpu.get_barrier_semaphore()

    def greet(day, space):
        pl.semaphore_signal(barrier, inc=1, device_id=(day, space), device_id_type=MESH)

    for link in to:
        greet(to[link], s)

    @pl.when(up_direct)
    def _():
        greet(d, s + 1)

    @pl.when(down_direct)
    def _():
        greet(d, s - 1)

    @pl.when(is_relay)
    def _():
        greet(partner, relay_from)

    @pl.when(is_edge)
    def _():
        for p in range(4):
            greet(partner, last_relay + 2 * p)

    lane = lax.broadcasted_iota(jnp.int32, (1, 128), 1) % 16
    right_half = jnp.where(lane >= 8, 1.0, 0.0).astype(BF16)
    left_half = jnp.where(lane < 8, 1.0, 0.0).astype(BF16)

    def cell_rows(src, first):
        for tb in range(3):
            for cp in range(2):
                x = jnp.concatenate(
                    [src[pl.ds(first + 16 * tb, 16), 2 * cp + c].reshape(256, 128) for c in range(2)], axis=1
                )
                w = dot(swap_ref[...], x).astype(BF16)
                for c in range(2):
                    for r in range(16):
                        row = ((2 * cp + c) * 2 + r // 8) * NA + 16 * tb
                        zbuf[pl.ds(row, 16), pl.ds((r % 8) * 128, 128)] = w[16 * r : 16 * r + 16, 128 * c : 128 * c + 128]

    def supercells(jp, put):
        o = dot(zbuf[...], cellm[:, pl.ds(256 * jp, 256)]).astype(BF16)
        for c in range(4):
            for half in range(2):
                row = (2 * c + half) * NA
                for jj in range(2):
                    put(half, 2 * jp + jj, c, o[row : row + NA, 128 * jj : 128 * jj + 128])

    bufs = (ga, gf)
    wide = (4, 2)

    def piece(arr, slot, p):
        if arr == 1 and p < 2:
            return f_left.at[p, slot]
        return bufs[arr].at[pl.ds(wide[arr] * p, wide[arr]), pl.ds(slot * NA, NA)]

    def remote(arr, link, src, dst, p):
        mine, there = piece(arr, src, p), piece(arr, dst, p)
        if arr == 1 and p == 0 and dst < 4:
            mine, there = mine.at[pl.ds(32, 16)], there.at[pl.ds(32, 16)]
        return pltpu.make_async_remote_copy(
            src_ref=mine, dst_ref=there,
            send_sem=gsend.at[arr, dst, p], recv_sem=grecv.at[arr, dst, p],
            device_id=(to[link], s), device_id_type=MESH,
        )

    def early(link, dst):
        return pltpu.make_async_remote_copy(
            src_ref=fin_hbm.at[pl.ds(0, 32), pl.ds(0, 16), pl.ds(0, 128)], dst_ref=f_left.at[0, dst, pl.ds(0, 32)],
            send_sem=esend.at[dst], recv_sem=erecv.at[dst],
            device_id=(to[link], s), device_id_type=MESH,
        )

    arrived = {(arr, 0, p) for arr in range(2) for p in range(4)}
    sent = []

    def need(arr, slot, p):
        if (arr, slot, p) not in arrived:
            arrived.add((arr, slot, p))
            remote(arr, "y", slot, slot, p).wait_recv()
            if arr == 1 and p == 0 and slot < 4:
                early("y", slot).wait_recv()

    def send(arr, link, src, dst, p):
        need(arr, src, p)
        copy = remote(arr, link, src, dst, p)
        copy.start()
        sent.append(copy)

    def blocks_of(k):
        return pl.ds(GROUPS[k][0], GROUPS[k][1] - GROUPS[k][0])

    def halo(row, k):
        there = s + 1 if row == 0 else s - 1
        return pltpu.make_async_remote_copy(
            src_ref=xs.at[row, blocks_of(k)], dst_ref=xr.at[row, blocks_of(k)],
            send_sem=xsend.at[row, k, 0], recv_sem=xrecv.at[row, k, 0],
            device_id=(d, there), device_id_type=MESH,
        )

    def halo_quarter(row, k, p):
        return pltpu.make_async_remote_copy(
            src_ref=xs.at[row, blocks_of(k), pl.ds(NA * p, NA)], dst_ref=relay.at[blocks_of(k)],
            send_sem=xsend.at[row, k, p], recv_sem=rrecv.at[k],
            device_id=(partner, first_relay + 2 * p), device_id_type=MESH,
        )

    def pass_on(row, k, p):
        if not isinstance(p, int):
            first = pl.multiple_of(NA * p, NA)
        else:
            first = NA * p
        return pltpu.make_async_remote_copy(
            src_ref=relay.at[blocks_of(k)], dst_ref=xr.at[row, blocks_of(k), pl.ds(first, NA)],
            send_sem=rsend.at[k], recv_sem=xrecv.at[row, k, p],
            device_id=(partner, relay_to), device_id_type=MESH,
        )

    def halo_start(k):
        for row, direct, edge in ((0, up_direct, 7), (1, down_direct, 8)):
            @pl.when(direct)
            def _():
                halo(row, k).start()

            @pl.when(s == edge)
            def _():
                for p in range(4):
                    halo_quarter(row, k, p).start()

    def halo_pass(k):
        for row in range(2):
            @pl.when(is_relay & (low if row == 0 else jnp.logical_not(low)))
            def _():
                halo_quarter(row, k, 0).wait_recv()
                pass_on(row, k, quarter).start()

    def halo_wait(k):
        for row, direct, edge in ((0, down_direct, 8), (1, up_direct, 7)):
            @pl.when(direct)
            def _():
                halo(row, k).wait_recv()

            @pl.when(s == edge)
            def _():
                for p in range(4):
                    pass_on(row, k, p).wait_recv()

    def halo_drain(k):
        for row, direct, edge in ((0, up_direct, 7), (1, down_direct, 8)):
            @pl.when(direct)
            def _():
                halo(row, k).wait_send()

            @pl.when(s == edge)
            def _():
                for p in range(4):
                    halo_quarter(row, k, p).wait_send()

        @pl.when(is_relay)
        def _():
            pass_on(0, k, quarter).wait_send()

    def scores(k):
        for slot in range(8):
            need(0, slot, k)

        @pl.loop(*GROUPS[k])
        def _(b):
            after = lax.rem(b + 1, NB)
            upper = dot_t(tf[b], ga[2 * b]) + dot_t(tf[b + 1], ga[2 * after])
            lower = dot_t(tf[9 + b], ga[2 * b + 1]) + dot_t(tf[10 + b], ga[2 * after + 1])
            own[b] = upper + lower
            xs[0, b] = lower
            xs[1, b] = upper

        halo_start(k)

    def weights(k):
        halo_wait(k)

        @pl.loop(*GROUPS[k])
        def _(b):
            for n in range(2):
                days = pl.ds(96 * n, 96)
                x = (own[b, days] + xr[0, b, days] + xr[1, b, days]) * (1.0 / 32.0)
                e = jnp.exp(x - jnp.max(x, axis=1, keepdims=True))
                wts[b, days] = e.astype(BF16)
                inv[b, days] = jnp.broadcast_to(1.0 / jnp.sum(e, axis=1, keepdims=True), (96, 128))

    def fine_blocks(src, side, slot):
        for tb in range(3):
            x = jnp.concatenate(
                [src[half, pl.ds(16 * tb, 16)].reshape(256, 128) for half in range(2)], axis=1
            )
            w = dot(swap_ref[...], x).astype(BF16)
            for half in range(2):
                for r in range(16):
                    g, i = (16 * half + r) // 4, r % 4
                    zbuf[pl.ds(NA * g + 16 * tb, 16), pl.ds(128 * i, 128)] = w[
                        16 * r : 16 * r + 16, 128 * half : 128 * half + 128
                    ]
        o = dot(zbuf[:, pl.ds(0, 512)], finem[...]).astype(BF16)
        for b in range(4):
            for g in range(8):
                gf[4 * side + b, pl.ds(NA * slot, NA), pl.ds(128 * g, 128)] = o[
                    NA * g : NA * g + NA, 128 * b : 128 * b + 128
                ]

    def lay(slot):
        need(1, slot, 0)
        need(1, slot, 1)
        fine_blocks(f_left.at[:, slot], 0, slot)

    def result(p):
        if p > 1:
            for slot in range(8):
                need(1, slot, p)

        @pl.loop(2 * p, 2 * p + 2)
        def _(b):
            scale = jnp.concatenate([inv[b], inv[b]], axis=1)
            for n in range(4):
                cols = pl.ds(256 * n, 256)
                res[b, :, cols] = (dot(wts[b], gf[b, :, cols]) * scale).astype(BF16)

        side = p // 2
        for g in range(8):
            x = jnp.concatenate([res[2 * p + b, :, pl.ds(128 * g, 128)] for b in range(2)], axis=1)
            o = dot(x, finem[pl.ds(256 * (p % 2), 256)]).astype(BF16)
            for i in range(4):
                v = o[:, 128 * i : 128 * i + 128]
                if p % 2:
                    v = v + rows[4 * g + i, :, pl.ds(128 * side, 128)]
                rows[4 * g + i, :, pl.ds(128 * side, 128)] = v

    def put_archive(half, j, c, v):
        ga[2 * j + half, pl.ds(0, NA), pl.ds(128 * c, 128)] = v

    pl.semaphore_wait(
        barrier,
        3 + up_direct.astype(jnp.int32) + down_direct.astype(jnp.int32)
        + is_relay.astype(jnp.int32) + 4 * is_edge.astype(jnp.int32),
    )
    for link, dst in (("y", 3), ("z+", 2), ("z-", 1)):
        copy = early(link, dst)
        copy.start()
        sent.append(copy)
    loads[0].wait()
    loads[1].wait()
    cell_rows(a_raw, 0)
    loads[2].wait()
    laid = set()
    for item in HEAD:
        if item[4] not in laid:
            laid.add(item[4])
            supercells(item[4], put_archive)
        send(*item)
    for p in range(4):
        if p not in laid:
            supercells(p, put_archive)

    for load in loads[3:8]:
        load.wait()
    fine_blocks(f_left.at[:, 0], 0, 0)
    fine_blocks(f_raw, 1, 0)

    loads[8].wait()

    def targets(lo, hi):
        @pl.loop(lo, hi)
        def _(n):
            first = pl.multiple_of(n * NA, NA)
            days = pl.ds(first, NA)

            def put(half, j, c, v):
                cols = pl.ds(128 * c, 128)
                if j:
                    tf[9 * half + j, days, cols] = v
                else:
                    tf[9 * half, days, cols] = v * right_half
                    tf[9 * half + 8, days, cols] = v * left_half

            cell_rows(t_raw, first)
            for jp in range(4):
                supercells(jp, put)

    targets(0, 2)
    for item in SENDS[:6]:
        send(*item)
    targets(2, 4)

    for row, edge in ((0, 0), (1, 15)):
        @pl.when(s == edge)
        def _():
            xr[row] = jnp.zeros(xr.shape[1:], F32)

    todo = {"scores": scores, "pass": halo_pass, "weights": weights, "lay": lay, "result": result}
    for item in SENDS[6:]:
        if isinstance(item, str):
            name, k = item.split()
            todo[name](int(k))
        else:
            send(*item)

    for k in range(4):
        halo_drain(k)
    for copy in sent:
        copy.wait_send()


def lay_out_kernel(rows_ref, swap_ref, out_hbm, laid, sems):
    stores = []
    for part in range(4):
        for tb in range(3 * part, 3 * part + 3):
            for half in range(2):
                x = rows_ref[pl.ds(16 * half, 16), pl.ds(16 * tb, 16)].reshape(256, 256)
                o = dot(swap_ref[...], x).astype(BF16)
                laid[pl.ds(16 * tb, 16), pl.ds(16 * half, 16)] = o.reshape(16, 16, 256)
        days = pl.ds(48 * part, 48)
        stores.append(pltpu.make_async_copy(laid.at[days], out_hbm.at[days], sems.at[part]))
        stores[-1].start()
    for store in stores:
        store.wait()


def on_device(targets, archive, archive_fine):
    swap = jnp.asarray(swap_matrix())
    cellm = jnp.asarray(cell_matrix())
    finem = jnp.asarray(fine_matrix())
    hbm = pl.BlockSpec(memory_space=pl.ANY)
    vmem = pl.BlockSpec(memory_space=pltpu.VMEM)
    dma = pltpu.SemaphoreType.DMA
    rows = pl.pallas_call(
        gather_kernel,
        out_shape=pltpu.VMEM((32, NT, 256), BF16),
        in_specs=[hbm] * 6,
        out_specs=vmem,
        scratch_shapes=[
            pltpu.VMEM((NT, 4, 16, 128), BF16),
            pltpu.VMEM((NA, 4, 16, 128), BF16),
            pltpu.VMEM((2, NA, 16, 128), BF16),
            pltpu.VMEM((2, 8, NA, 16, 128), BF16),
            pltpu.VMEM((256, 256), BF16),
            pltpu.VMEM((1024, 1024), BF16),
            pltpu.VMEM((512, 512), BF16),
            pltpu.VMEM((16, ALL, 512), BF16),
            pltpu.VMEM((NB, ALL, 1024), BF16),
            pltpu.VMEM((18, NT, 512), BF16),
            pltpu.VMEM((8 * NA, 1024), BF16),
            pltpu.VMEM((NB, NT, ALL), F32),
            pltpu.VMEM((2, NB, NT, ALL), F32),
            pltpu.VMEM((2, NB, NT, ALL), F32),
            pltpu.VMEM((NB, NA, ALL), F32),
            pltpu.VMEM((NB, NT, ALL), BF16),
            pltpu.VMEM((NB, NT, 128), F32),
            pltpu.VMEM((NB, NT, 1024), BF16),
            dma((9,)), dma((2, 8, 4)), dma((2, 8, 4)),
            dma((2, 4, 4)), dma((2, 4, 4)), dma((4,)), dma((4,)), dma((4,)), dma((4,)),
        ],
        compiler_params=pltpu.CompilerParams(
            collective_id=0, has_side_effects=True, vmem_limit_bytes=56 << 20
        ),
        cost_estimate=pl.CostEstimate(flops=6_000_000_000, bytes_accessed=16_000_000, transcendentals=600_000),
    )(*[
        pltpu.with_memory_space_constraint(x, pltpu.HBM)
        for x in (targets, archive, archive_fine, swap, cellm, finem)
    ])
    return pl.pallas_call(
        lay_out_kernel,
        out_shape=jax.ShapeDtypeStruct((NT, 32, 256), BF16),
        in_specs=[vmem, vmem],
        out_specs=hbm,
        scratch_shapes=[pltpu.VMEM((NT, 32, 256), BF16), dma((4,))],
        compiler_params=pltpu.CompilerParams(vmem_limit_bytes=32 << 20),
        cost_estimate=pl.CostEstimate(flops=800_000_000, bytes_accessed=6_300_000, transcendentals=0),
    )(rows, swap)


def solution(mesh):
    return jax.shard_map(
        on_device,
        mesh=mesh,
        in_specs=(
            P("days", None, "space", None),
            P("days", None, "space", None),
            P("days", "space", None),
        ),
        out_specs=P("days", "space", None),
        check_vma=False,
    )
```

```python
import functools

import jax
import jax.numpy as jnp
import ml_dtypes
import numpy as np
from jax import lax
from jax.experimental import pallas as pl
from jax.experimental.pallas import tpu as pltpu
from jax.sharding import PartitionSpec as P

MESH = pl.DeviceIdType.MESH
BF16, F32 = jnp.bfloat16, jnp.float32

NT, NA, NB = 192, 48, 8
ALL = 8 * NA

HEAD = [
    (0, "y", 0, 3, 0), (0, "z+", 0, 2, 1), (0, "z-", 0, 1, 0), (0, "y", 0, 3, 1), (0, "z+", 0, 2, 0),
    (0, "z-", 0, 1, 2), (0, "y", 1, 4, 0), (0, "z+", 0, 2, 3), (0, "z-", 1, 6, 0),
]
SENDS = [
    (0, "y", 2, 5, 1), (0, "z+", 3, 5, 0), (0, "z-", 0, 1, 1), (0, "y", 0, 3, 2), (0, "z+", 2, 6, 1),
    (0, "z-", 4, 7, 0), (0, "y", 1, 4, 2), (0, "z+", 5, 7, 1), (1, "z-", 0, 1, 0), (0, "z-", 3, 4, 1),
    "scores 0", (1, "y", 0, 3, 0), (1, "z+", 0, 2, 1), (0, "y", 2, 5, 3), (0, "z-", 0, 1, 3),
    (0, "z+", 0, 2, 2), "scores 1", (0, "z-", 1, 6, 2), (1, "y", 1, 4, 0), (0, "z+", 3, 5, 2), "pass 0",
    (0, "z-", 4, 7, 2), (0, "y", 0, 3, 3), (0, "z+", 2, 6, 3), (1, "z-", 1, 6, 0), "pass 1", (0, "y", 1, 4, 3),
    (0, "z+", 5, 7, 3), "scores 2", (1, "z-", 4, 7, 0), (1, "y", 0, 3, 1), (1, "z+", 0, 2, 0),
    (1, "z+", 0, 2, 3), (1, "z-", 0, 1, 2), "scores 3", (1, "y", 2, 5, 1), "lay 2", (1, "z+", 3, 5, 0),
    (1, "z-", 0, 1, 1), "weights 0", "lay 3", "pass 2", (1, "z+", 2, 6, 1), (1, "z-", 3, 4, 1),
    (1, "y", 1, 4, 2), "weights 1", "lay 1", (1, "z+", 5, 7, 1), "lay 5", (1, "z-", 0, 1, 3), "pass 3",
    (1, "y", 0, 3, 2), (1, "z+", 0, 2, 2), "lay 4", "lay 6", (1, "z-", 1, 6, 2), (1, "y", 2, 5, 3), "lay 7",
    "result 0", "weights 2", "result 1", (1, "z-", 4, 7, 2), (1, "z+", 3, 5, 2), (1, "y", 0, 3, 3),
    (1, "z-", 1, 6, 3), (1, "z+", 5, 7, 3), (1, "y", 1, 4, 3), "weights 3", "result 2", "result 3",
]
GROUPS = [(0, 1), (1, 3), (3, 5), (5, 8)]


def swap_matrix():
    m = np.zeros((16, 16, 16, 16), np.float32)
    for r in range(16):
        for t in range(16):
            m[r, t, t, r] = 1
    return m.reshape(256, 256).astype(ml_dtypes.bfloat16)


def cell_matrix():
    m = np.zeros((8, 128, 8, 8, 16), np.float32)
    for r in range(8):
        for j in range(8):
            for q in range(16):
                m[r, (16 * j - 8 + q) % 128, j, r, q] = 1
    return m.reshape(1024, 1024).astype(ml_dtypes.bfloat16)


def fine_matrix():
    m = np.zeros((4, 4, 32, 4, 4, 32), np.float32)
    for i in range(4):
        for b in range(4):
            for q in range(32):
                m[i, b, q, b, i, q] = 1
    return m.reshape(512, 512).astype(ml_dtypes.bfloat16)


def dot(a, b):
    return jnp.dot(a, b, preferred_element_type=F32)


def dot_t(a, b):
    return lax.dot_general(a, b, (((1,), (1,)), ((), ())), preferred_element_type=F32)


def gather_kernel(
    tgt_hbm, arc_hbm, fin_hbm, swap_hbm, cellm_hbm, finem_hbm, rows,
    t_raw, a_raw, f_raw, f_left, swap_ref, cellm, finem, ga, gf, tf, zbuf, own, xs, xr, relay, wts, inv, res,
    lsem, gsend, grecv, xsend, xrecv, rsend, rrecv, esend, erecv,
):
    d = lax.axis_index("days")
    s = lax.axis_index("space")
    z, y = d // 2, d % 2
    partner = 2 * z + 1 - y
    to = {"y": partner, "z+": 2 * lax.rem(z + 1, 4) + y, "z-": 2 * lax.rem(z + 3, 4) + y}

    up_direct = (s != 7) & (s != 15)
    down_direct = (s != 0) & (s != 8)
    is_edge = (s == 7) | (s == 8)
    low = s < 8
    is_relay = (low & (s % 2 == 1)) | (jnp.logical_not(low) & (s % 2 == 0))
    relay_to = jnp.where(low, 8, 7)
    relay_from = jnp.where(low, 7, 8)
    quarter = (s % 8) // 2
    first_relay = jnp.where(low, 1, 8)
    last_relay = jnp.where(low, 8, 1)

    loads = [
        pltpu.make_async_copy(src, dst, lsem.at[i])
        for i, (src, dst) in enumerate(
            [
                (arc_hbm, a_raw), (swap_hbm, swap_ref), (cellm_hbm, cellm),
                (finem_hbm, finem),
                (fin_hbm.at[:, pl.ds(0, 16), pl.ds(0, 128)], f_left.at[0, 0]),
                (fin_hbm.at[:, pl.ds(16, 16), pl.ds(0, 128)], f_left.at[1, 0]),
                (fin_hbm.at[:, pl.ds(0, 16), pl.ds(128, 128)], f_raw.at[0]),
                (fin_hbm.at[:, pl.ds(16, 16), pl.ds(128, 128)], f_raw.at[1]),
                (tgt_hbm, t_raw),
            ]
        )
    ]
    for load in loads:
        load.start()

    barrier = pltpu.get_barrier_semaphore()

    def greet(day, space):
        pl.semaphore_signal(barrier, inc=1, device_id=(day, space), device_id_type=MESH)

    for link in to:
        greet(to[link], s)

    @pl.when(up_direct)
    def _():
        greet(d, s + 1)

    @pl.when(down_direct)
    def _():
        greet(d, s - 1)

    @pl.when(is_relay)
    def _():
        greet(partner, relay_from)

    @pl.when(is_edge)
    def _():
        for p in range(4):
            greet(partner, last_relay + 2 * p)

    lane = lax.broadcasted_iota(jnp.int32, (1, 128), 1) % 16
    right_half = jnp.where(lane >= 8, 1.0, 0.0).astype(BF16)
    left_half = jnp.where(lane < 8, 1.0, 0.0).astype(BF16)

    def cell_rows(src, first):
        for tb in range(3):
            for cp in range(2):
                x = jnp.concatenate(
                    [src[pl.ds(first + 16 * tb, 16), 2 * cp + c].reshape(256, 128) for c in range(2)], axis=1
                )
                w = dot(swap_ref[...], x).astype(BF16)
                for c in range(2):
                    for r in range(16):
                        row = ((2 * cp + c) * 2 + r // 8) * NA + 16 * tb
                        zbuf[pl.ds(row, 16), pl.ds((r % 8) * 128, 128)] = w[16 * r : 16 * r + 16, 128 * c : 128 * c + 128]

    def supercells(jp, put):
        o = dot(zbuf[...], cellm[:, pl.ds(256 * jp, 256)]).astype(BF16)
        for c in range(4):
            for half in range(2):
                row = (2 * c + half) * NA
                for jj in range(2):
                    put(half, 2 * jp + jj, c, o[row : row + NA, 128 * jj : 128 * jj + 128])

    bufs = (ga, gf)
    wide = (4, 2)

    def piece(arr, slot, p):
        if arr == 1 and p < 2:
            return f_left.at[p, slot]
        return bufs[arr].at[pl.ds(wide[arr] * p, wide[arr]), pl.ds(slot * NA, NA)]

    def remote(arr, link, src, dst, p):
        mine, there = piece(arr, src, p), piece(arr, dst, p)
        if arr == 1 and p == 0 and dst < 4:
            mine, there = mine.at[pl.ds(32, 16)], there.at[pl.ds(32, 16)]
        return pltpu.make_async_remote_copy(
            src_ref=mine, dst_ref=there,
            send_sem=gsend.at[arr, dst, p], recv_sem=grecv.at[arr, dst, p],
            device_id=(to[link], s), device_id_type=MESH,
        )

    def early(link, dst):
        return pltpu.make_async_remote_copy(
            src_ref=fin_hbm.at[pl.ds(0, 32), pl.ds(0, 16), pl.ds(0, 128)], dst_ref=f_left.at[0, dst, pl.ds(0, 32)],
            send_sem=esend.at[dst], recv_sem=erecv.at[dst],
            device_id=(to[link], s), device_id_type=MESH,
        )

    arrived = {(arr, 0, p) for arr in range(2) for p in range(4)}
    sent = []

    def need(arr, slot, p):
        if (arr, slot, p) not in arrived:
            arrived.add((arr, slot, p))
            remote(arr, "y", slot, slot, p).wait_recv()
            if arr == 1 and p == 0 and slot < 4:
                early("y", slot).wait_recv()

    def send(arr, link, src, dst, p):
        need(arr, src, p)
        copy = remote(arr, link, src, dst, p)
        copy.start()
        sent.append(copy)

    def blocks_of(k):
        return pl.ds(GROUPS[k][0], GROUPS[k][1] - GROUPS[k][0])

    def halo(row, k):
        there = s + 1 if row == 0 else s - 1
        return pltpu.make_async_remote_copy(
            src_ref=xs.at[row, blocks_of(k)], dst_ref=xr.at[row, blocks_of(k)],
            send_sem=xsend.at[row, k, 0], recv_sem=xrecv.at[row, k, 0],
            device_id=(d, there), device_id_type=MESH,
        )

    def halo_quarter(row, k, p):
        return pltpu.make_async_remote_copy(
            src_ref=xs.at[row, blocks_of(k), pl.ds(NA * p, NA)], dst_ref=relay.at[blocks_of(k)],
            send_sem=xsend.at[row, k, p], recv_sem=rrecv.at[k],
            device_id=(partner, first_relay + 2 * p), device_id_type=MESH,
        )

    def pass_on(row, k, p):
        if not isinstance(p, int):
            first = pl.multiple_of(NA * p, NA)
        else:
            first = NA * p
        return pltpu.make_async_remote_copy(
            src_ref=relay.at[blocks_of(k)], dst_ref=xr.at[row, blocks_of(k), pl.ds(first, NA)],
            send_sem=rsend.at[k], recv_sem=xrecv.at[row, k, p],
            device_id=(partner, relay_to), device_id_type=MESH,
        )

    def halo_start(k):
        for row, direct, edge in ((0, up_direct, 7), (1, down_direct, 8)):
            @pl.when(direct)
            def _():
                halo(row, k).start()

            @pl.when(s == edge)
            def _():
                for p in range(4):
                    halo_quarter(row, k, p).start()

    def halo_pass(k):
        for row in range(2):
            @pl.when(is_relay & (low if row == 0 else jnp.logical_not(low)))
            def _():
                halo_quarter(row, k, 0).wait_recv()
                pass_on(row, k, quarter).start()

    def halo_wait(k):
        for row, direct, edge in ((0, down_direct, 8), (1, up_direct, 7)):
            @pl.when(direct)
            def _():
                halo(row, k).wait_recv()

            @pl.when(s == edge)
            def _():
                for p in range(4):
                    pass_on(row, k, p).wait_recv()

    def halo_drain(k):
        for row, direct, edge in ((0, up_direct, 7), (1, down_direct, 8)):
            @pl.when(direct)
            def _():
                halo(row, k).wait_send()

            @pl.when(s == edge)
            def _():
                for p in range(4):
                    halo_quarter(row, k, p).wait_send()

        @pl.when(is_relay)
        def _():
            pass_on(0, k, quarter).wait_send()

    def scores(k):
        for slot in range(8):
            need(0, slot, k)

        @pl.loop(*GROUPS[k])
        def _(b):
            after = lax.rem(b + 1, NB)
            upper = dot_t(tf[b], ga[2 * b]) + dot_t(tf[b + 1], ga[2 * after])
            lower = dot_t(tf[9 + b], ga[2 * b + 1]) + dot_t(tf[10 + b], ga[2 * after + 1])
            own[b] = upper + lower
            xs[0, b] = lower
            xs[1, b] = upper

        halo_start(k)

    def weights(k):
        halo_wait(k)

        @pl.loop(*GROUPS[k])
        def _(b):
            for n in range(2):
                days = pl.ds(96 * n, 96)
                x = (own[b, days] + xr[0, b, days] + xr[1, b, days]) * (1.0 / 32.0)
                e = jnp.exp(x - jnp.max(x, axis=1, keepdims=True))
                wts[b, days] = e.astype(BF16)
                inv[b, days] = jnp.broadcast_to(1.0 / jnp.sum(e, axis=1, keepdims=True), (96, 128))

    def fine_blocks(src, side, slot):
        for tb in range(3):
            x = jnp.concatenate(
                [src[half, pl.ds(16 * tb, 16)].reshape(256, 128) for half in range(2)], axis=1
            )
            w = dot(swap_ref[...], x).astype(BF16)
            for half in range(2):
                for r in range(16):
                    g, i = (16 * half + r) // 4, r % 4
                    zbuf[pl.ds(NA * g + 16 * tb, 16), pl.ds(128 * i, 128)] = w[
                        16 * r : 16 * r + 16, 128 * half : 128 * half + 128
                    ]
        o = dot(zbuf[:, pl.ds(0, 512)], finem[...]).astype(BF16)
        for b in range(4):
            for g in range(8):
                gf[4 * side + b, pl.ds(NA * slot, NA), pl.ds(128 * g, 128)] = o[
                    NA * g : NA * g + NA, 128 * b : 128 * b + 128
                ]

    def lay(slot):
        need(1, slot, 0)
        need(1, slot, 1)
        fine_blocks(f_left.at[:, slot], 0, slot)

    def result(p):
        if p > 1:
            for slot in range(8):
                need(1, slot, p)

        @pl.loop(2 * p, 2 * p + 2)
        def _(b):
            scale = jnp.concatenate([inv[b], inv[b]], axis=1)
            for n in range(4):
                cols = pl.ds(256 * n, 256)
                res[b, :, cols] = (dot(wts[b], gf[b, :, cols]) * scale).astype(BF16)

        side = p // 2
        for g in range(8):
            x = jnp.concatenate([res[2 * p + b, :, pl.ds(128 * g, 128)] for b in range(2)], axis=1)
            o = dot(x, finem[pl.ds(256 * (p % 2), 256)]).astype(BF16)
            for i in range(4):
                v = o[:, 128 * i : 128 * i + 128]
                if p % 2:
                    v = v + rows[4 * g + i, :, pl.ds(128 * side, 128)]
                rows[4 * g + i, :, pl.ds(128 * side, 128)] = v

    def put_archive(half, j, c, v):
        ga[2 * j + half, pl.ds(0, NA), pl.ds(128 * c, 128)] = v

    pl.semaphore_wait(
        barrier,
        3 + up_direct.astype(jnp.int32) + down_direct.astype(jnp.int32)
        + is_relay.astype(jnp.int32) + 4 * is_edge.astype(jnp.int32),
    )
    for link, dst in (("y", 3), ("z+", 2), ("z-", 1)):
        copy = early(link, dst)
        copy.start()
        sent.append(copy)
    loads[0].wait()
    loads[1].wait()
    cell_rows(a_raw, 0)
    loads[2].wait()
    laid = set()
    for item in HEAD:
        if item[4] not in laid:
            laid.add(item[4])
            supercells(item[4], put_archive)
        send(*item)
    for p in range(4):
        if p not in laid:
            supercells(p, put_archive)

    for load in loads[3:8]:
        load.wait()
    fine_blocks(f_left.at[:, 0], 0, 0)
    fine_blocks(f_raw, 1, 0)

    loads[8].wait()

    def targets(lo, hi):
        @pl.loop(lo, hi)
        def _(n):
            first = pl.multiple_of(n * NA, NA)
            days = pl.ds(first, NA)

            def put(half, j, c, v):
                cols = pl.ds(128 * c, 128)
                if j:
                    tf[9 * half + j, days, cols] = v
                else:
                    tf[9 * half, days, cols] = v * right_half
                    tf[9 * half + 8, days, cols] = v * left_half

            cell_rows(t_raw, first)
            for jp in range(4):
                supercells(jp, put)

    targets(0, 2)
    for item in SENDS[:6]:
        send(*item)
    targets(2, 4)

    for row, edge in ((0, 0), (1, 15)):
        @pl.when(s == edge)
        def _():
            xr[row] = jnp.zeros(xr.shape[1:], F32)

    todo = {"scores": scores, "pass": halo_pass, "weights": weights, "lay": lay, "result": result}
    for item in SENDS[6:]:
        if isinstance(item, str):
            name, k = item.split()
            todo[name](int(k))
        else:
            send(*item)

    for k in range(4):
        halo_drain(k)
    for copy in sent:
        copy.wait_send()


def lay_out_kernel(rows_ref, swap_ref, out_hbm, laid, sems):
    stores = []
    for part in range(4):
        for tb in range(3 * part, 3 * part + 3):
            for half in range(2):
                x = rows_ref[pl.ds(16 * half, 16), pl.ds(16 * tb, 16)].reshape(256, 256)
                o = dot(swap_ref[...], x).astype(BF16)
                laid[pl.ds(16 * tb, 16), pl.ds(16 * half, 16)] = o.reshape(16, 16, 256)
        days = pl.ds(48 * part, 48)
        stores.append(pltpu.make_async_copy(laid.at[days], out_hbm.at[days], sems.at[part]))
        stores[-1].start()
    for store in stores:
        store.wait()


def on_device(targets, archive, archive_fine):
    swap = jnp.asarray(swap_matrix())
    cellm = jnp.asarray(cell_matrix())
    finem = jnp.asarray(fine_matrix())
    hbm = pl.BlockSpec(memory_space=pl.ANY)
    vmem = pl.BlockSpec(memory_space=pltpu.VMEM)
    dma = pltpu.SemaphoreType.DMA
    rows = pl.pallas_call(
        gather_kernel,
        out_shape=pltpu.VMEM((32, NT, 256), BF16),
        in_specs=[hbm] * 6,
        out_specs=vmem,
        scratch_shapes=[
            pltpu.VMEM((NT, 4, 16, 128), BF16),
            pltpu.VMEM((NA, 4, 16, 128), BF16),
            pltpu.VMEM((2, NA, 16, 128), BF16),
            pltpu.VMEM((2, 8, NA, 16, 128), BF16),
            pltpu.VMEM((256, 256), BF16),
            pltpu.VMEM((1024, 1024), BF16),
            pltpu.VMEM((512, 512), BF16),
            pltpu.VMEM((16, ALL, 512), BF16),
            pltpu.VMEM((NB, ALL, 1024), BF16),
            pltpu.VMEM((18, NT, 512), BF16),
            pltpu.VMEM((8 * NA, 1024), BF16),
            pltpu.VMEM((NB, NT, ALL), F32),
            pltpu.VMEM((2, NB, NT, ALL), F32),
            pltpu.VMEM((2, NB, NT, ALL), F32),
            pltpu.VMEM((NB, NA, ALL), F32),
            pltpu.VMEM((NB, NT, ALL), BF16),
            pltpu.VMEM((NB, NT, 128), F32),
            pltpu.VMEM((NB, NT, 1024), BF16),
            dma((9,)), dma((2, 8, 4)), dma((2, 8, 4)),
            dma((2, 4, 4)), dma((2, 4, 4)), dma((4,)), dma((4,)), dma((4,)), dma((4,)),
        ],
        compiler_params=pltpu.CompilerParams(
            collective_id=0, has_side_effects=True, vmem_limit_bytes=56 << 20
        ),
        cost_estimate=pl.CostEstimate(flops=6_000_000_000, bytes_accessed=16_000_000, transcendentals=600_000),
    )(*[
        pltpu.with_memory_space_constraint(x, pltpu.HBM)
        for x in (targets, archive, archive_fine, swap, cellm, finem)
    ])
    return pl.pallas_call(
        lay_out_kernel,
        out_shape=jax.ShapeDtypeStruct((NT, 32, 256), BF16),
        in_specs=[vmem, vmem],
        out_specs=hbm,
        scratch_shapes=[pltpu.VMEM((NT, 32, 256), BF16), dma((4,))],
        compiler_params=pltpu.CompilerParams(vmem_limit_bytes=32 << 20),
        cost_estimate=pl.CostEstimate(flops=800_000_000, bytes_accessed=6_300_000, transcendentals=0),
    )(rows, swap)


def solution(mesh):
    return jax.shard_map(
        on_device,
        mesh=mesh,
        in_specs=(
            P("days", None, "space", None),
            P("days", None, "space", None),
            P("days", "space", None),
        ),
        out_specs=P("days", "space", None),
        check_vma=False,
    )
```
